32 devices in a mesh: groups: 2 (over x), row: 16 (over z, y, core).
Axes of the slice: x: 2, y: 2, z: 4, core: 2. Of those that a mesh axis runs over, the one named last changes fastest.
Arguments:
- matrix_a: float32 [6144, 1024], P(('groups', 'row')), parts along dimension 0, may hold values from -2.16506351 to 2.16506351, as said below
- matrix_b: float32 [6144, 1024], P(('groups', 'row')), parts along dimension 0, may hold values from -6 to 6
Outputs:
- first_factor: float32 [2048, 1024], P(('groups', 'row')), parts along dimension 0
- factor: float32 [2048, 1024], P(('groups', 'row')), parts along dimension 0
- projection: float32 [2048, 1024], P(('groups', 'row')), parts along dimension 0
The draws below stay inside these ranges and needn't reach their ends.
There are 2 independent parts, one for each index of `groups`. The reference program is written for one: setup_inputs(seed, part) draws one part's arguments, and reference() takes and returns one part's arrays. A program takes and returns all parts, laid end to end along the dimension named above; each array names one. Nothing has to cross between parts.
Inputs may be any that keep to these rules, and one draw needn't show every extreme that they name: `matrix_a`: A real matrix of full column rank.
All inputs are finite; a program needn't handle non-finite values.
Results may differ from the reference program's by a relative error of at most 0.0003.
Values sent between devices are 32-bit elements; how exact they have to be, the bound alone decides.
A program may use at most 128 MiB of HBM per device.

```python
import math
import jax
import jax.numpy as jnp
from jax import lax

N = 1024
ROWS = 3072


def draw_matrix_a(key, part):
    keys = jax.random.split(jax.random.fold_in(key, 7), 5)
    position = jnp.arange(ROWS, dtype=jnp.float32) / ROWS
    jitter = jax.random.uniform(keys[1], (ROWS,), jnp.float32, -0.05, 0.05)
    top = 4.0
    spread = 0.25
    level = 0.05
    noise = jnp.clip(jax.random.normal(keys[0], (ROWS, N), jnp.float32), -6.0, 6.0)
    column_scale = 10.0 ** jax.random.uniform(keys[2], (N,), jnp.float32, -spread, spread)
    components = min(128, N // 2)
    weights = 0.9 ** jnp.arange(components, dtype=jnp.float32)
    weight_norm = jnp.sqrt(jnp.sum(weights * weights))
    left = jax.random.uniform(keys[3], (ROWS, components), jnp.float32, -1.732, 1.732)
    right = jax.random.uniform(keys[4], (components, N), jnp.float32, -1.732, 1.732)
    shared = jnp.dot(left * weights[None, :], right, precision=lax.Precision.HIGHEST, preferred_element_type=jnp.float32) / weight_norm
    row_scale = top ** (position + jitter)
    mean_square = (top * top - 1.0) / (2.0 * math.log(top))
    shared = shared * (row_scale[:, None] / math.sqrt(mean_square))
    return (shared + level * noise) * column_scale[None, :] / math.sqrt(ROWS)


def block_levels(own_key, shape, cuts, low, top_value):
    gain = 1.0
    for dim, blocks in cuts:
        steps = jax.random.uniform(jax.random.fold_in(jax.random.fold_in(own_key, 6), dim), (blocks,), jnp.float32, low / len(cuts), top_value / len(cuts))
        gain = gain * jnp.repeat(jnp.exp(steps), shape[dim] // blocks).reshape((-1,) + (1,) * (len(shape) - 1 - dim))
    return gain


def normal_values(own_key, extent, scale, limit, cuts=(), kind=jnp.bfloat16):
    factor_of = block_levels(own_key, extent, cuts, -0.22, 0.18) if cuts else 1.0
    values = jax.random.normal(own_key, extent, jnp.float32) * scale * factor_of
    return jnp.minimum(jnp.maximum(values, -limit), limit).astype(kind)


def setup_inputs(seed: int = 0, part: int = 0) -> dict:
    splits = jax.random.split(jax.random.key(seed), 3)
    part_keys = jax.random.split(jax.random.fold_in(splits[2], part), 3)
    return {
        "matrix_a": draw_matrix_a(jax.random.fold_in(jax.random.fold_in(splits[2], part), 71), part),
        "matrix_b": normal_values(part_keys[1], (ROWS, N), 1.0, 6.0, ((0, 16),), jnp.float32),
    }


def reference(matrix_a, matrix_b):
    highest = lax.Precision.HIGHEST
    gram1 = jnp.dot(matrix_a.T.astype(jnp.float32), matrix_a.astype(jnp.float32), precision=highest, preferred_element_type=jnp.float32)
    shift = jnp.trace(gram1) / (4.0 * N)
    lower1 = jnp.linalg.cholesky(gram1 + shift * jnp.eye(N, dtype=jnp.float32))
    basis1 = lax.linalg.triangular_solve(lower1, matrix_a, left_side=False, lower=True, transpose_a=True)
    gram2 = jnp.dot(basis1.T.astype(jnp.float32), basis1.astype(jnp.float32), precision=highest, preferred_element_type=jnp.float32)
    lower2 = jnp.linalg.cholesky(gram2)
    basis = lax.linalg.triangular_solve(lower2, basis1, left_side=False, lower=True, transpose_a=True)
    factor = jnp.dot(lower2.T.astype(jnp.float32), lower1.T.astype(jnp.float32), precision=highest, preferred_element_type=jnp.float32)
    projection = jnp.dot(basis.T.astype(jnp.float32), matrix_b.astype(jnp.float32), precision=highest, preferred_element_type=jnp.float32)
    return (lower1.T, factor, projection)
```

```python
import functools
import math

import jax
import jax.numpy as jnp
from jax import lax
from jax.experimental import pallas as pl
from jax.experimental.pallas import tpu as pltpu
from jax.sharding import PartitionSpec as P

HIGHEST = lax.Precision.HIGHEST
PANEL = 8


def mm(x, y, dims):
    return lax.dot_general(
        x, y, (dims, ((), ())), precision=HIGHEST, preferred_element_type=jnp.float32
    )


def spread(row, shape):
    return jnp.broadcast_to(row, shape)


def factor_block(rows, size):
    shape = (PANEL, size)
    lane = lax.broadcasted_iota(jnp.int32, shape, 1)
    sub = lax.broadcasted_iota(jnp.int32, shape, 0)
    rows = list(rows)
    upper, lower = [], []
    for p in range(size // PANEL):
        first = p * PANEL
        inside = (lane >= first) & (lane < first + PANEL)
        right = lane >= first + PANEL
        panel = rows[p]
        cols = [spread(panel[:, first + c : first + c + 1], shape) for c in range(PANEL)]
        panel = jnp.where(inside, jnp.where(lane - first == sub, 1.0, 0.0), panel)
        pivots = jnp.ones(shape, jnp.float32)
        inverse = jnp.ones(shape, jnp.float32)
        for t in range(PANEL):
            pivot = spread(cols[t][t : t + 1, :], shape)
            one_over = 1.0 / pivot
            pivots = jnp.where(sub == t, pivot, pivots)
            inverse = jnp.where(sub == t, one_over, inverse)
            if t + 1 < PANEL:
                mult = jnp.where(sub > t, cols[t] * one_over, 0.0)
                for c in range(t + 1, PANEL):
                    cols[c] = cols[c] - mult * spread(cols[c][t : t + 1, :], shape)
                panel = panel - mult * spread(panel[t : t + 1, :], shape)
        if first + PANEL < size:
            weights = jnp.where(right, panel * inverse, 0.0)
            update = mm(weights, panel, ((0,), (0,)))
            for q in range(p + 1, size // PANEL):
                kept = jnp.where(inside, 0.0, rows[q])
                rows[q] = kept - update[q * PANEL : (q + 1) * PANEL]
        scale = 1.0 / jnp.sqrt(pivots)
        corner = jnp.zeros(shape, jnp.float32)
        for c in range(PANEL):
            corner = jnp.where((lane == first + c) & (sub <= c), cols[c], corner)
        upper.append(jnp.where(right, panel, corner) * scale)
        lower.append(jnp.where(right, 0.0, panel) * scale)
    return jnp.concatenate(upper, axis=0), jnp.concatenate(lower, axis=0)


def factor_kernel(block, g_ref, r_ref, t_ref, pan):
    width = g_ref.shape[0]
    blocks = width // block
    t_ref[...] = g_ref[...]
    column = lax.broadcasted_iota(jnp.int32, (block, width), 1)

    def step(k, carry):
        begin = pl.multiple_of(k * block, block)
        own = pl.ds(begin, block)
        rows = [
            t_ref[pl.ds(pl.multiple_of(begin + p * PANEL, PANEL), PANEL), own]
            for p in range(block // PANEL)
        ]
        upper, lower = factor_block(rows, block)
        pan[...] = mm(lower, t_ref[own, :], ((1,), (0,)))
        pan[:, own] = lower

        def trail(i, inner):
            other = pl.ds(pl.multiple_of(i * block, block), block)
            t_ref[other, own] = jnp.zeros((block, block), jnp.float32)
            t_ref[other, :] = t_ref[other, :] - mm(pan[:, other], pan[...], ((0,), (0,)))
            return inner

        lax.fori_loop(k + 1, blocks, trail, 0)
        after = column >= begin + block
        r_ref[own, :] = jnp.where(after, pan[...], 0.0)
        r_ref[own, own] = upper
        t_ref[own, :] = jnp.where(after, 0.0, pan[...])
        return carry

    lax.fori_loop(0, blocks, step, 0)


def factor_pair(gram):
    width = gram.shape[0]
    block = math.gcd(width, 128)
    whole = jax.ShapeDtypeStruct((width, width), jnp.float32)
    return pl.pallas_call(
        functools.partial(factor_kernel, block),
        out_shape=(whole, whole),
        in_specs=[pl.BlockSpec(memory_space=pltpu.VMEM)],
        out_specs=(pl.BlockSpec(memory_space=pltpu.VMEM),) * 2,
        scratch_shapes=[pltpu.VMEM((block, width), jnp.float32)],
        compiler_params=pltpu.CompilerParams(vmem_limit_bytes=40 * 1024 * 1024),
        cost_estimate=pl.CostEstimate(
            flops=100 * width**3, bytes_accessed=12 * width * width, transcendentals=0
        ),
    )(gram)


def per_device(matrix_a, matrix_b):
    width = matrix_a.shape[1]
    out_rows = width // lax.axis_size("row")
    start = lax.axis_index("row") * out_rows
    gram1 = lax.psum(mm(matrix_a, matrix_a, ((0,), (0,))), "row")
    cross = mm(matrix_a, matrix_b, ((0,), (0,)))
    gram1, cross = lax.optimization_barrier((gram1, cross))
    cross = lax.psum(cross, "row")
    shift = jnp.trace(gram1) / (4.0 * width)
    upper1, inverse1 = factor_pair(gram1 + shift * jnp.eye(width, dtype=jnp.float32))
    inverse1, cross = lax.optimization_barrier((inverse1, cross))
    basis1 = mm(matrix_a, inverse1, ((1,), (1,)))
    gram2 = lax.psum(mm(basis1, basis1, ((0,), (0,))), "row")
    partial = mm(inverse1, cross, ((1,), (0,)))
    upper2, inverse2 = factor_pair(gram2)
    first_rows = lax.dynamic_slice_in_dim(upper1, start, out_rows, 0)
    second_rows = lax.dynamic_slice_in_dim(upper2, start, out_rows, 0)
    inverse_rows = lax.dynamic_slice_in_dim(inverse2, start, out_rows, 0)
    factor_rows = mm(second_rows, upper1, ((1,), (0,)))
    projection = mm(inverse_rows, partial, ((1,), (0,)))
    return (first_rows, factor_rows, projection)


def solution(mesh):
    placed = P(("groups", "row"), None)
    return jax.shard_map(
        per_device,
        mesh=mesh,
        in_specs=(placed, placed),
        out_specs=(placed, placed, placed),
        check_vma=False,
    )
```

```python
import functools
import math

import jax
import jax.numpy as jnp
from jax import lax
from jax.experimental import pallas as pl
from jax.experimental.pallas import tpu as pltpu
from jax.sharding import PartitionSpec as P

HIGHEST = lax.Precision.HIGHEST
PANEL = 8


def mm(x, y, dims):
    return lax.dot_general(
        x, y, (dims, ((), ())), precision=HIGHEST, preferred_element_type=jnp.float32
    )


def spread(row, shape):
    return jnp.broadcast_to(row, shape)


def factor_block(rows, size):
    shape = (PANEL, size)
    lane = lax.broadcasted_iota(jnp.int32, shape, 1)
    sub = lax.broadcasted_iota(jnp.int32, shape, 0)
    rows = list(rows)
    upper, lower = [], []
    for p in range(size // PANEL):
        first = p * PANEL
        inside = (lane >= first) & (lane < first + PANEL)
        right = lane >= first + PANEL
        panel = rows[p]
        cols = [spread(panel[:, first + c : first + c + 1], shape) for c in range(PANEL)]
        panel = jnp.where(inside, jnp.where(lane - first == sub, 1.0, 0.0), panel)
        pivots = jnp.ones(shape, jnp.float32)
        inverse = jnp.ones(shape, jnp.float32)
        for t in range(PANEL):
            pivot = spread(cols[t][t : t + 1, :], shape)
            one_over = 1.0 / pivot
            pivots = jnp.where(sub == t, pivot, pivots)
            inverse = jnp.where(sub == t, one_over, inverse)
            if t + 1 < PANEL:
                mult = jnp.where(sub > t, cols[t] * one_over, 0.0)
                for c in range(t + 1, PANEL):
                    cols[c] = cols[c] - mult * spread(cols[c][t : t + 1, :], shape)
                panel = panel - mult * spread(panel[t : t + 1, :], shape)
        if first + PANEL < size:
            weights = jnp.where(right, panel * inverse, 0.0)
            update = mm(weights, panel, ((0,), (0,)))
            for q in range(p + 1, size // PANEL):
                kept = jnp.where(inside, 0.0, rows[q])
                rows[q] = kept - update[q * PANEL : (q + 1) * PANEL]
        scale = 1.0 / jnp.sqrt(pivots)
        corner = jnp.zeros(shape, jnp.float32)
        for c in range(PANEL):
            corner = jnp.where((lane == first + c) & (sub <= c), cols[c], corner)
        upper.append(jnp.where(right, panel, corner) * scale)
        lower.append(jnp.where(right, 0.0, panel) * scale)
    return jnp.concatenate(upper, axis=0), jnp.concatenate(lower, axis=0)


def factor_kernel(block, g_ref, r_ref, t_ref, pan):
    width = g_ref.shape[0]
    blocks = width // block
    t_ref[...] = g_ref[...]
    column = lax.broadcasted_iota(jnp.int32, (block, width), 1)

    def step(k, carry):
        begin = pl.multiple_of(k * block, block)
        own = pl.ds(begin, block)
        rows = [
            t_ref[pl.ds(pl.multiple_of(begin + p * PANEL, PANEL), PANEL), own]
            for p in range(block // PANEL)
        ]
        upper, lower = factor_block(rows, block)
        pan[...] = mm(lower, t_ref[own, :], ((1,), (0,)))
        pan[:, own] = lower

        def trail(i, inner):
            other = pl.ds(pl.multiple_of(i * block, block), block)
            t_ref[other, own] = jnp.zeros((block, block), jnp.float32)
            t_ref[other, :] = t_ref[other, :] - mm(pan[:, other], pan[...], ((0,), (0,)))
            return inner

        lax.fori_loop(k + 1, blocks, trail, 0)
        after = column >= begin + block
        r_ref[own, :] = jnp.where(after, pan[...], 0.0)
        r_ref[own, own] = upper
        t_ref[own, :] = jnp.where(after, 0.0, pan[...])
        return carry

    lax.fori_loop(0, blocks, step, 0)


def factor_pair(gram):
    width = gram.shape[0]
    block = math.gcd(width, 128)
    whole = jax.ShapeDtypeStruct((width, width), jnp.float32)
    return pl.pallas_call(
        functools.partial(factor_kernel, block),
        out_shape=(whole, whole),
        in_specs=[pl.BlockSpec(memory_space=pltpu.VMEM)],
        out_specs=(pl.BlockSpec(memory_space=pltpu.VMEM),) * 2,
        scratch_shapes=[pltpu.VMEM((block, width), jnp.float32)],
        compiler_params=pltpu.CompilerParams(vmem_limit_bytes=40 * 1024 * 1024),
        cost_estimate=pl.CostEstimate(
            flops=100 * width**3, bytes_accessed=12 * width * width, transcendentals=0
        ),
    )(gram)


def sum_kernel(orders, x_ref, out_ref, *scratch):
    lanes, steps = len(orders), len(orders[0])
    slots = [scratch[lane * steps : (lane + 1) * steps] for lane in range(lanes)]
    down_send, down_recv, up_send, up_recv = scratch[lanes * steps :]
    me = lax.axis_index("row")
    share = x_ref.shape[0] // lanes
    bits = [lax.rem(me // (1 << b), 2) for b in range(steps)]
    partners = [me + (1 - 2 * bits[b]) * (1 << b) for b in range(steps)]

    barrier = pltpu.get_barrier_semaphore()
    for partner in partners:
        pl.semaphore_signal(
            barrier, inc=1, device_id={"row": partner}, device_id_type=pl.DeviceIdType.MESH
        )
    pl.semaphore_wait(barrier, steps)

    def source(lane, step):
        return x_ref.at[pl.ds(lane * share, share)] if step == 0 else slots[lane][step - 1]

    def halve(lane, step):
        bit = orders[lane][step]
        size = share >> (step + 1)
        copy = pltpu.make_async_remote_copy(
            src_ref=source(lane, step).at[pl.ds((1 - bits[bit]) * size, size)],
            dst_ref=slots[lane][step],
            send_sem=down_send.at[lane, step],
            recv_sem=down_recv.at[lane, step],
            device_id={"row": partners[bit]},
            device_id_type=pl.DeviceIdType.MESH,
        )
        copy.start()
        return copy

    def offset(lane, level):
        total = lane * share
        for step in range(level):
            total = total + bits[orders[lane][step]] * (share >> (step + 1))
        return total

    def double(lane, step):
        bit = orders[lane][step]
        own = pl.ds(offset(lane, step + 1), share >> (step + 1))
        copy = pltpu.make_async_remote_copy(
            src_ref=out_ref.at[own],
            dst_ref=out_ref.at[own],
            send_sem=up_send.at[lane, step],
            recv_sem=up_recv.at[lane, step],
            device_id={"row": partners[bit]},
            device_id_type=pl.DeviceIdType.MESH,
        )
        copy.start()
        return copy

    flying = [halve(lane, 0) for lane in range(lanes)]
    for step in range(steps):
        for lane in range(lanes):
            flying[lane].wait()
            size = share >> (step + 1)
            kept = source(lane, step)[pl.ds(bits[orders[lane][step]] * size, size)]
            if step + 1 < steps:
                slots[lane][step][...] = slots[lane][step][...] + kept
                flying[lane] = halve(lane, step + 1)
            else:
                out_ref[pl.ds(offset(lane, steps), size)] = slots[lane][step][...] + kept
                flying[lane] = double(lane, steps - 1)
    for step in range(steps - 1, -1, -1):
        for lane in range(lanes):
            flying[lane].wait()
            if step > 0:
                flying[lane] = double(lane, step - 1)


def sum_tiles(tiles, devices):
    steps = devices.bit_length() - 1
    straight = list(range(steps))
    orders = (straight, straight[:1] + straight[2:] + straight[1:2])
    share = tiles.shape[0] // len(orders)
    slots = [
        pltpu.VMEM((share >> (step + 1),) + tiles.shape[1:], jnp.float32)
        for _ in orders
        for step in range(steps)
    ]
    sems = [pltpu.SemaphoreType.DMA((len(orders), steps))] * 4
    return pl.pallas_call(
        functools.partial(sum_kernel, orders),
        out_shape=jax.ShapeDtypeStruct(tiles.shape, jnp.float32),
        in_specs=[pl.BlockSpec(memory_space=pltpu.VMEM)],
        out_specs=pl.BlockSpec(memory_space=pltpu.VMEM),
        scratch_shapes=slots + sems,
        compiler_params=pltpu.CompilerParams(
            collective_id=0, has_side_effects=True, vmem_limit_bytes=24 * 1024 * 1024
        ),
        cost_estimate=pl.CostEstimate(
            flops=1 << 33, bytes_accessed=8 * tiles.size, transcendentals=0
        ),
    )(tiles)


def to_tiles(x):
    rows, columns = x.shape
    return x.reshape(rows // 8, 8, columns // 128, 128).swapaxes(1, 2).reshape(-1, 8, 128)


def from_tiles(x, columns):
    return x.reshape(-1, columns // 128, 8, 128).swapaxes(1, 2).reshape(-1, columns)


def sum_gram(basis):
    devices = lax.axis_size("row")
    width = basis.shape[1]
    half = width // 2
    if devices & (devices - 1) or devices < 4 or width % 256:
        return lax.psum(mm(basis, basis, ((0,), (0,))), "row")
    left, right = basis[:, :half], basis[:, half:]
    top = mm(left, basis, ((0,), (0,)))
    bottom = mm(right, right, ((0,), (0,)))
    row = lax.broadcasted_iota(jnp.int32, (half, half), 0)
    col = lax.broadcasted_iota(jnp.int32, (half, half), 1)
    folded = jnp.where(row <= col, top[:, :half], bottom)
    extra = 8
    while (half + extra) // 8 * (width // 128) % (2 * devices):
        extra += 8
    ends = jnp.pad(jnp.diagonal(bottom)[None, :], ((0, extra - 1), (0, width - half)))
    packed = jnp.concatenate([jnp.concatenate([folded, top[:, half:]], axis=1), ends], axis=0)
    packed = from_tiles(sum_tiles(to_tiles(packed), devices), width)
    folded, corner, ends = packed[:half, :half], packed[:half, half:], packed[half, :half]
    turned = folded.T
    first = jnp.where(row <= col, folded, turned)
    second = jnp.where(row == col, ends[None, :], jnp.where(row > col, folded, turned))
    return jnp.concatenate(
        [
            jnp.concatenate([first, corner], axis=1),
            jnp.concatenate([jnp.zeros_like(corner), second], axis=1),
        ],
        axis=0,
    )


def per_device(matrix_a, matrix_b):
    width = matrix_a.shape[1]
    out_rows = width // lax.axis_size("row")
    start = lax.axis_index("row") * out_rows
    gram1 = sum_gram(matrix_a)
    cross = mm(matrix_a, matrix_b, ((0,), (0,)))
    gram1, cross = lax.optimization_barrier((gram1, cross))
    cross = lax.psum(cross, "row")
    shift = jnp.trace(gram1) / (4.0 * width)
    upper1, inverse1 = factor_pair(gram1 + shift * jnp.eye(width, dtype=jnp.float32))
    basis1 = mm(matrix_a, inverse1, ((1,), (1,)))
    gram2 = sum_gram(basis1)
    upper2, inverse2 = factor_pair(gram2)
    first_rows = lax.dynamic_slice_in_dim(upper1, start, out_rows, 0)
    second_rows = lax.dynamic_slice_in_dim(upper2, start, out_rows, 0)
    inverse_rows = lax.dynamic_slice_in_dim(inverse2, start, out_rows, 0)
    factor_rows = mm(second_rows, upper1, ((1,), (0,)))
    inverse_rows = mm(inverse_rows, inverse1, ((1,), (0,)))
    projection = mm(inverse_rows, cross, ((1,), (0,)))
    return (first_rows, factor_rows, projection)


def solution(mesh):
    placed = P(("groups", "row"), None)
    return jax.shard_map(
        per_device,
        mesh=mesh,
        in_specs=(placed, placed),
        out_specs=(placed, placed, placed),
        check_vma=False,
    )
```

```python
import functools

import jax
import jax.numpy as jnp
from jax import lax
from jax.experimental import pallas as pl
from jax.experimental.pallas import tpu as pltpu
from jax.sharding import PartitionSpec as P

HIGHEST = lax.Precision.HIGHEST
PANEL = 8
LANES = 128


def mm(x, y, dims):
    return lax.dot_general(
        x, y, (dims, ((), ())), precision=HIGHEST, preferred_element_type=jnp.float32
    )


def spread(row, shape):
    return jnp.broadcast_to(row, shape)


def factor_block(rows, size):
    shape = (PANEL, size)
    lane = lax.broadcasted_iota(jnp.int32, shape, 1)
    sub = lax.broadcasted_iota(jnp.int32, shape, 0)
    rows = list(rows)
    upper, lower = [], []
    for p in range(size // PANEL):
        first = p * PANEL
        inside = (lane >= first) & (lane < first + PANEL)
        right = lane >= first + PANEL
        panel = rows[p]
        cols = [spread(panel[:, first + c : first + c + 1], shape) for c in range(PANEL)]
        ahead = p + 1 < size // PANEL
        if ahead:
            follow = rows[p + 1]
            under = [spread(follow[:, first + c : first + c + 1], shape) for c in range(PANEL)]
            follow = jnp.where(inside, 0.0, follow)
        panel = jnp.where(inside, jnp.where(lane - first == sub, 1.0, 0.0), panel)
        pivots = jnp.ones(shape, jnp.float32)
        inverse = jnp.ones(shape, jnp.float32)
        for t in range(PANEL):
            pivot = spread(cols[t][t : t + 1, :], shape)
            one_over = 1.0 / pivot
            pivots = jnp.where(sub == t, pivot, pivots)
            inverse = jnp.where(sub == t, one_over, inverse)
            mult = jnp.where(sub > t, cols[t] * one_over, 0.0)
            whole = spread(panel[t : t + 1, :], shape)
            heads = [spread(cols[c][t : t + 1, :], shape) for c in range(t + 1, PANEL)]
            for c, head in zip(range(t + 1, PANEL), heads):
                cols[c] = cols[c] - mult * head
            panel = panel - mult * whole
            if ahead:
                low = under[t] * one_over
                for c, head in zip(range(t + 1, PANEL), heads):
                    under[c] = under[c] - low * head
                follow = follow - low * whole
        if ahead:
            rows[p + 1] = follow
        if p + 2 < size // PANEL:
            weights = jnp.where(right, panel * inverse, 0.0)
            update = mm(weights, panel, ((0,), (0,)))
            for q in range(p + 2, size // PANEL):
                kept = jnp.where(inside, 0.0, rows[q])
                rows[q] = kept - update[q * PANEL : (q + 1) * PANEL]
        scale = 1.0 / jnp.sqrt(pivots)
        corner = jnp.zeros(shape, jnp.float32)
        for c in range(PANEL):
            corner = jnp.where((lane == first + c) & (sub <= c), cols[c], corner)
        upper.append(jnp.where(right, panel, corner) * scale)
        lower.append(jnp.where(right, 0.0, panel) * scale)
    return jnp.concatenate(upper, axis=0), jnp.concatenate(lower, axis=0)


def unfold(x_ref, t_ref, width, shifted):
    half, parts = width // 2, width // (2 * LANES)
    row = lax.broadcasted_iota(jnp.int32, (LANES, LANES), 0)
    col = lax.broadcasted_iota(jnp.int32, (LANES, LANES), 1)
    tiles = LANES // 8

    def place(i, j, value):
        t_ref[i * LANES : (i + 1) * LANES, j * LANES : (j + 1) * LANES] = value

    for i in range(2 * parts):
        for j in range(i):
            place(i, j, jnp.zeros((LANES, LANES), jnp.float32))
    trace = jnp.zeros((1, 1), jnp.float32)
    for i in range(parts):
        for j in range(2 * parts):
            value = x_ref[i * tiles : (i + 1) * tiles, j].reshape(LANES, LANES)
            if j >= parts or i < j:
                place(i, j, value)
            elif i > j:
                place(parts + j, parts + i, value.T)
            else:
                turned = value.T
                ends = x_ref[half // 8, j][0:1, :]
                place(i, i, jnp.where(row <= col, value, turned))
                lower = jnp.where(row > col, value, turned)
                place(parts + i, parts + i, jnp.where(row == col, ends, lower))
                if shifted:
                    pivots = jnp.where(row == col, value + ends, 0.0)
                    line = jnp.sum(pivots, axis=0, keepdims=True)
                    trace = trace + jnp.sum(line, axis=1, keepdims=True)
    if shifted:
        shift = trace * (1.0 / (4.0 * width))
        for i in range(2 * parts):
            own = slice(i * LANES, (i + 1) * LANES)
            t_ref[own, own] = t_ref[own, own] + jnp.where(row == col, shift, 0.0)


def factor_kernel(block, shifted, x_ref, r_ref, t_ref, pan):
    width = t_ref.shape[0]
    blocks = width // block
    unfold(x_ref, t_ref, width, shifted)
    column = lax.broadcasted_iota(jnp.int32, (block, width), 1)

    def step(k, carry):
        begin = pl.multiple_of(k * block, block)
        own = pl.ds(begin, block)
        rows = [
            t_ref[pl.ds(pl.multiple_of(begin + p * PANEL, PANEL), PANEL), own]
            for p in range(block // PANEL)
        ]
        upper, lower = factor_block(rows, block)
        pan[...] = mm(lower, t_ref[own, :], ((1,), (0,)))
        pan[:, own] = lower

        def trail(i, inner):
            other = pl.ds(pl.multiple_of(i * block, block), block)
            t_ref[other, own] = jnp.zeros((block, block), jnp.float32)
            t_ref[other, :] = t_ref[other, :] - mm(pan[:, other], pan[...], ((0,), (0,)))
            return inner

        lax.fori_loop(k + 1, blocks, trail, 0)
        after = column >= begin + block
        r_ref[own, :] = jnp.where(after, pan[...], 0.0)
        r_ref[own, own] = upper
        t_ref[own, :] = jnp.where(after, 0.0, pan[...])
        return carry

    lax.fori_loop(0, blocks, step, 0)


def factor_pair(folded, width, shifted):
    whole = jax.ShapeDtypeStruct((width, width), jnp.float32)
    return pl.pallas_call(
        functools.partial(factor_kernel, LANES, shifted),
        out_shape=(whole, whole),
        in_specs=[pl.BlockSpec(memory_space=pltpu.VMEM)],
        out_specs=(pl.BlockSpec(memory_space=pltpu.VMEM),) * 2,
        scratch_shapes=[pltpu.VMEM((LANES, width), jnp.float32)],
        compiler_params=pltpu.CompilerParams(vmem_limit_bytes=40 * 1024 * 1024),
        cost_estimate=pl.CostEstimate(
            flops=100 * width**3, bytes_accessed=12 * width * width, transcendentals=0
        ),
    )(folded)


def gram_kernel(basis_ref, x_ref):
    width = basis_ref.shape[1]
    half, parts = width // 2, width // (2 * LANES)
    tiles = LANES // 8
    row = lax.broadcasted_iota(jnp.int32, (LANES, LANES), 0)
    col = lax.broadcasted_iota(jnp.int32, (LANES, LANES), 1)
    x_ref[half // 8 :] = jnp.zeros((x_ref.shape[0] - half // 8,) + x_ref.shape[1:], jnp.float32)
    for i in range(parts):
        left = basis_ref[:, i * LANES : (i + 1) * LANES]
        right = basis_ref[:, half + i * LANES : half + (i + 1) * LANES]
        upper = mm(left, basis_ref[:, i * LANES :], ((0,), (0,)))
        lower = mm(right, basis_ref[:, half : half + (i + 1) * LANES], ((0,), (0,)))
        for j in range(2 * parts):
            if j >= i:
                above = upper[:, (j - i) * LANES : (j - i + 1) * LANES]
            if j <= i:
                below = lower[:, j * LANES : (j + 1) * LANES]
            if j == i:
                value = jnp.where(row <= col, above, below)
                line = jnp.sum(jnp.where(row == col, below, 0.0), axis=0, keepdims=True)
                x_ref[half // 8, j, 0:1, :] = line
            else:
                value = above if j > i else below
            x_ref[i * tiles : (i + 1) * tiles, j] = value.reshape(tiles, 8, LANES)


def folded_gram(basis, devices):
    width = basis.shape[1]
    lanes = width // LANES
    count = width // 16 + 1
    while count * lanes % (2 * devices):
        count += 1
    return pl.pallas_call(
        gram_kernel,
        out_shape=jax.ShapeDtypeStruct((count, lanes, 8, LANES), jnp.float32),
        in_specs=[pl.BlockSpec(memory_space=pltpu.VMEM)],
        out_specs=pl.BlockSpec(memory_space=pltpu.VMEM),
        compiler_params=pltpu.CompilerParams(vmem_limit_bytes=24 * 1024 * 1024),
        cost_estimate=pl.CostEstimate(
            flops=12 * basis.shape[0] * width**2, bytes_accessed=8 * basis.size, transcendentals=0
        ),
    )(basis)


def sum_kernel(orders, x_ref, out_ref, *scratch):
    lanes, steps = len(orders), len(orders[0])
    slots = [scratch[lane * steps : (lane + 1) * steps] for lane in range(lanes)]
    down_send, down_recv, up_send, up_recv = scratch[lanes * steps :]
    me = lax.axis_index("row")
    share = x_ref.shape[0] // lanes
    bits = [lax.rem(me // (1 << b), 2) for b in range(steps)]
    partners = [me + (1 - 2 * bits[b]) * (1 << b) for b in range(steps)]

    barrier = pltpu.get_barrier_semaphore()
    for partner in partners:
        pl.semaphore_signal(
            barrier, inc=1, device_id={"row": partner}, device_id_type=pl.DeviceIdType.MESH
        )
    pl.semaphore_wait(barrier, steps)

    def source(lane, step):
        return x_ref.at[pl.ds(lane * share, share)] if step == 0 else slots[lane][step - 1]

    def halve(lane, step):
        bit = orders[lane][step]
        size = share >> (step + 1)
        copy = pltpu.make_async_remote_copy(
            src_ref=source(lane, step).at[pl.ds((1 - bits[bit]) * size, size)],
            dst_ref=slots[lane][step],
            send_sem=down_send.at[lane, step],
            recv_sem=down_recv.at[lane, step],
            device_id={"row": partners[bit]},
            device_id_type=pl.DeviceIdType.MESH,
        )
        copy.start()
        return copy

    def offset(lane, level):
        total = lane * share
        for step in range(level):
            total = total + bits[orders[lane][step]] * (share >> (step + 1))
        return total

    def double(lane, step):
        bit = orders[lane][step]
        own = pl.ds(offset(lane, step + 1), share >> (step + 1))
        copy = pltpu.make_async_remote_copy(
            src_ref=out_ref.at[own],
            dst_ref=out_ref.at[own],
            send_sem=up_send.at[lane, step],
            recv_sem=up_recv.at[lane, step],
            device_id={"row": partners[bit]},
            device_id_type=pl.DeviceIdType.MESH,
        )
        copy.start()
        return copy

    flying = [halve(lane, 0) for lane in range(lanes)]
    for step in range(steps):
        for lane in range(lanes):
            flying[lane].wait()
            size = share >> (step + 1)
            kept = source(lane, step)[pl.ds(bits[orders[lane][step]] * size, size)]
            if step + 1 < steps:
                slots[lane][step][...] = slots[lane][step][...] + kept
                flying[lane] = halve(lane, step + 1)
            else:
                out_ref[pl.ds(offset(lane, steps), size)] = slots[lane][step][...] + kept
                flying[lane] = double(lane, steps - 1)
    for step in range(steps - 1, -1, -1):
        for lane in range(lanes):
            flying[lane].wait()
            if step > 0:
                flying[lane] = double(lane, step - 1)


def sum_tiles(tiles, devices):
    steps = devices.bit_length() - 1
    straight = list(range(steps))
    orders = (straight, straight[:1] + straight[2:] + straight[1:2])
    share = tiles.shape[0] // len(orders)
    slots = [
        pltpu.VMEM((share >> (step + 1),) + tiles.shape[1:], jnp.float32)
        for _ in orders
        for step in range(steps)
    ]
    sems = [pltpu.SemaphoreType.DMA((len(orders), steps))] * 4
    return pl.pallas_call(
        functools.partial(sum_kernel, orders),
        out_shape=jax.ShapeDtypeStruct(tiles.shape, jnp.float32),
        in_specs=[pl.BlockSpec(memory_space=pltpu.VMEM)],
        out_specs=pl.BlockSpec(memory_space=pltpu.VMEM),
        scratch_shapes=slots + sems,
        compiler_params=pltpu.CompilerParams(
            collective_id=0, has_side_effects=True, vmem_limit_bytes=24 * 1024 * 1024
        ),
        cost_estimate=pl.CostEstimate(
            flops=1 << 33, bytes_accessed=8 * tiles.size, transcendentals=0
        ),
    )(tiles)


def sum_gram(basis):
    devices = lax.axis_size("row")
    folded = folded_gram(basis, devices)
    return sum_tiles(folded.reshape(-1, 8, LANES), devices).reshape(folded.shape)


def per_device(matrix_a, matrix_b):
    width = matrix_a.shape[1]
    out_rows = width // lax.axis_size("row")
    start = lax.axis_index("row") * out_rows
    gram1 = sum_gram(matrix_a)
    cross = mm(matrix_a, matrix_b, ((0,), (0,)))
    gram1, cross = lax.optimization_barrier((gram1, cross))
    cross = lax.psum(cross, "row")
    upper1, inverse1 = factor_pair(gram1, width, True)
    basis1 = mm(matrix_a, inverse1, ((1,), (1,)))
    gram2 = sum_gram(basis1)
    upper2, inverse2 = factor_pair(gram2, width, False)
    first_rows = lax.dynamic_slice_in_dim(upper1, start, out_rows, 0)
    second_rows = lax.dynamic_slice_in_dim(upper2, start, out_rows, 0)
    inverse_rows = lax.dynamic_slice_in_dim(inverse2, start, out_rows, 0)
    factor_rows = mm(second_rows, upper1, ((1,), (0,)))
    inverse_rows = mm(inverse_rows, inverse1, ((1,), (0,)))
    projection = mm(inverse_rows, cross, ((1,), (0,)))
    return (first_rows, factor_rows, projection)


def solution(mesh):
    placed = P(("groups", "row"), None)
    return jax.shard_map(
        per_device,
        mesh=mesh,
        in_specs=(placed, placed),
        out_specs=(placed, placed, placed),
        check_vma=False,
    )
```

```python
import functools

import jax
import jax.numpy as jnp
from jax import lax
from jax.experimental import pallas as pl
from jax.experimental.pallas import tpu as pltpu
from jax.sharding import PartitionSpec as P

HIGHEST = lax.Precision.HIGHEST
PANEL = 8
LANES = 128


def mm(x, y, dims):
    return lax.dot_general(
        x, y, (dims, ((), ())), precision=HIGHEST, preferred_element_type=jnp.float32
    )


def spread(row, shape):
    return jnp.broadcast_to(row, shape)


def factor_block(rows, size, beside):
    shape = (PANEL, size)
    lane = lax.broadcasted_iota(jnp.int32, shape, 1)
    sub = lax.broadcasted_iota(jnp.int32, shape, 0)
    rows = list(rows)
    upper, lower = [], []
    for p in range(size // PANEL):
        first = p * PANEL
        inside = (lane >= first) & (lane < first + PANEL)
        right = lane >= first + PANEL
        panel = rows[p]
        cols = [spread(panel[:, first + c : first + c + 1], shape) for c in range(PANEL)]
        ahead = p + 1 < size // PANEL
        if ahead:
            follow = rows[p + 1]
            under = [spread(follow[:, first + c : first + c + 1], shape) for c in range(PANEL)]
            follow = jnp.where(inside, 0.0, follow)
        panel = jnp.where(inside, jnp.where(lane - first == sub, 1.0, 0.0), panel)
        beside(p)
        pivots = jnp.ones(shape, jnp.float32)
        inverse = jnp.ones(shape, jnp.float32)
        for t in range(PANEL):
            pivot = spread(cols[t][t : t + 1, :], shape)
            one_over = 1.0 / pivot
            pivots = jnp.where(sub == t, pivot, pivots)
            inverse = jnp.where(sub == t, one_over, inverse)
            mult = jnp.where(sub > t, cols[t] * one_over, 0.0)
            whole = spread(panel[t : t + 1, :], shape)
            heads = [spread(cols[c][t : t + 1, :], shape) for c in range(t + 1, PANEL)]
            for c, head in zip(range(t + 1, PANEL), heads):
                cols[c] = cols[c] - mult * head
            panel = panel - mult * whole
            if ahead:
                low = under[t] * one_over
                for c, head in zip(range(t + 1, PANEL), heads):
                    under[c] = under[c] - low * head
                follow = follow - low * whole
        if ahead:
            rows[p + 1] = follow
        if p + 2 < size // PANEL:
            weights = jnp.where(right, panel * inverse, 0.0)
            update = mm(weights, panel, ((0,), (0,)))
            for q in range(p + 2, size // PANEL):
                kept = jnp.where(inside, 0.0, rows[q])
                rows[q] = kept - update[q * PANEL : (q + 1) * PANEL]
        scale = 1.0 / jnp.sqrt(pivots)
        corner = jnp.zeros(shape, jnp.float32)
        for c in range(PANEL):
            corner = jnp.where((lane == first + c) & (sub <= c), cols[c], corner)
        upper.append(jnp.where(right, panel, corner) * scale)
        lower.append(jnp.where(right, 0.0, panel) * scale)
    return jnp.concatenate(upper, axis=0), jnp.concatenate(lower, axis=0)


def unfold(x_ref, t_ref, width, shifted):
    half, parts = width // 2, width // (2 * LANES)
    row = lax.broadcasted_iota(jnp.int32, (LANES, LANES), 0)
    col = lax.broadcasted_iota(jnp.int32, (LANES, LANES), 1)
    tiles = LANES // 8

    def place(i, j, value):
        t_ref[i * LANES : (i + 1) * LANES, j * LANES : (j + 1) * LANES] = value

    for i in range(2 * parts):
        for j in range(i):
            place(i, j, jnp.zeros((LANES, LANES), jnp.float32))
    trace = jnp.zeros((1, 1), jnp.float32)
    for i in range(parts):
        for j in range(2 * parts):
            value = x_ref[i * tiles : (i + 1) * tiles, j].reshape(LANES, LANES)
            if j >= parts or i < j:
                place(i, j, value)
            elif i > j:
                place(parts + j, parts + i, value.T)
            else:
                turned = value.T
                ends = x_ref[half // 8, j][0:1, :]
                place(i, i, jnp.where(row <= col, value, turned))
                lower = jnp.where(row > col, value, turned)
                place(parts + i, parts + i, jnp.where(row == col, ends, lower))
                if shifted:
                    pivots = jnp.where(row == col, value + ends, 0.0)
                    line = jnp.sum(pivots, axis=0, keepdims=True)
                    trace = trace + jnp.sum(line, axis=1, keepdims=True)
    if shifted:
        shift = trace * (1.0 / (4.0 * width))
        for i in range(2 * parts):
            own = slice(i * LANES, (i + 1) * LANES)
            t_ref[own, own] = t_ref[own, own] + jnp.where(row == col, shift, 0.0)


def factor_kernel(block, shifted, x_ref, r_ref, t_ref, work, pans):
    width = t_ref.shape[0]
    blocks = width // block
    turns = block // PANEL
    piece = width * (blocks - 1) // turns // LANES * LANES
    while piece == 0 or width % piece or (width // piece) * (blocks - 1) > turns:
        piece += LANES
    pieces = width // piece
    unfold(x_ref, work, width, shifted)
    pans[1] = jnp.zeros(pans.shape[1:], jnp.float32)
    pans[0, :, width:] = jnp.zeros((block, block), jnp.float32)
    work[width:, :] = jnp.zeros((block, width), jnp.float32)
    column = lax.broadcasted_iota(jnp.int32, (block, width), 1)
    part = lax.broadcasted_iota(jnp.int32, (block, piece), 1)

    def step(k, carry):
        begin = pl.multiple_of(k * block, block)
        own = pl.ds(begin, block)
        now, before = lax.rem(k, 2), lax.rem(k + 1, 2)

        def beside(p):
            if p >= pieces * (blocks - 1):
                return
            target = jnp.minimum(k + 1 + p // pieces, blocks)
            other = pl.ds(pl.multiple_of(target * block, block), block)
            low = p % pieces * piece
            place = slice(low, low + piece)
            gone = (part + low >= begin - block) & (part + low < begin)
            update = mm(pans[before, :, other], pans[before, :, place], ((0,), (0,)))
            work[other, place] = jnp.where(gone, 0.0, work[other, place]) - update

        rows = [
            work[pl.ds(pl.multiple_of(begin + p * PANEL, PANEL), PANEL), own]
            for p in range(turns)
        ]
        upper, lower = factor_block(rows, block, beside)
        pans[now, :, :width] = mm(lower, work[own, :], ((1,), (0,)))
        pans[now, :, own] = lower
        pan = pans[now, :, :width]
        after = column >= begin + block
        following = pl.ds(pl.multiple_of(begin + block, block), block)
        gone = (column >= begin) & (column < begin + block)
        update = mm(pans[now, :, following], pan, ((0,), (0,)))
        work[following, :] = jnp.where(gone, 0.0, work[following, :]) - update
        r_ref[own, :] = jnp.where(after, pan, 0.0)
        r_ref[own, own] = upper
        t_ref[own, :] = jnp.where(after, 0.0, pan)
        return carry

    lax.fori_loop(0, blocks, step, 0)


def factor_pair(folded, width, shifted):
    whole = jax.ShapeDtypeStruct((width, width), jnp.float32)
    return pl.pallas_call(
        functools.partial(factor_kernel, LANES, shifted),
        out_shape=(whole, whole),
        in_specs=[pl.BlockSpec(memory_space=pltpu.VMEM)],
        out_specs=(pl.BlockSpec(memory_space=pltpu.VMEM),) * 2,
        scratch_shapes=[
            pltpu.VMEM((width + LANES, width), jnp.float32),
            pltpu.VMEM((2, LANES, width + LANES), jnp.float32),
        ],
        compiler_params=pltpu.CompilerParams(vmem_limit_bytes=32 * 1024 * 1024),
        cost_estimate=pl.CostEstimate(
            flops=100 * width**3, bytes_accessed=12 * width * width, transcendentals=0
        ),
    )(folded)


def basis_kernel(a_ref, inverse_ref, x_ref, basis):
    basis[...] = mm(a_ref[...], inverse_ref[...], ((1,), (1,)))
    gram_kernel(basis, x_ref)


def gram_kernel(basis_ref, x_ref):
    width = basis_ref.shape[1]
    half, parts = width // 2, width // (2 * LANES)
    tiles = LANES // 8
    row = lax.broadcasted_iota(jnp.int32, (LANES, LANES), 0)
    col = lax.broadcasted_iota(jnp.int32, (LANES, LANES), 1)
    x_ref[half // 8 :] = jnp.zeros((x_ref.shape[0] - half // 8,) + x_ref.shape[1:], jnp.float32)
    for i in range(parts):
        left = basis_ref[:, i * LANES : (i + 1) * LANES]
        right = basis_ref[:, half + i * LANES : half + (i + 1) * LANES]
        upper = mm(left, basis_ref[:, i * LANES :], ((0,), (0,)))
        lower = mm(right, basis_ref[:, half : half + (i + 1) * LANES], ((0,), (0,)))
        for j in range(2 * parts):
            if j >= i:
                above = upper[:, (j - i) * LANES : (j - i + 1) * LANES]
            if j <= i:
                below = lower[:, j * LANES : (j + 1) * LANES]
            if j == i:
                value = jnp.where(row <= col, above, below)
                line = jnp.sum(jnp.where(row == col, below, 0.0), axis=0, keepdims=True)
                x_ref[half // 8, j, 0:1, :] = line
            else:
                value = above if j > i else below
            x_ref[i * tiles : (i + 1) * tiles, j] = value.reshape(tiles, 8, LANES)


def folded_gram(basis, devices, inverse=None):
    width = basis.shape[1]
    lanes = width // LANES
    count = width // 16 + 1
    while count * lanes % (2 * devices):
        count += 1
    operands = (basis,) if inverse is None else (basis, inverse)
    return pl.pallas_call(
        gram_kernel if inverse is None else basis_kernel,
        out_shape=jax.ShapeDtypeStruct((count, lanes, 8, LANES), jnp.float32),
        in_specs=[pl.BlockSpec(memory_space=pltpu.VMEM)] * len(operands),
        out_specs=pl.BlockSpec(memory_space=pltpu.VMEM),
        scratch_shapes=[] if inverse is None else [pltpu.VMEM(basis.shape, jnp.float32)],
        compiler_params=pltpu.CompilerParams(vmem_limit_bytes=24 * 1024 * 1024),
        cost_estimate=pl.CostEstimate(
            flops=12 * basis.shape[0] * width**2, bytes_accessed=8 * basis.size, transcendentals=0
        ),
    )(*operands)


def cross_kernel(a_ref, b_ref, c_ref):
    for i in range(a_ref.shape[1] // LANES):
        own = slice(i * LANES, (i + 1) * LANES)
        c_ref[own, :] = mm(a_ref[:, own], b_ref[...], ((0,), (0,)))


def tail_kernel(second_ref, rows_ref, upper_ref, inverse_ref, cross_ref, factor_ref, out_ref):
    factor_ref[...] = mm(second_ref[...], upper_ref[...], ((1,), (0,)))
    rows = mm(rows_ref[...], inverse_ref[...], ((1,), (0,)))
    out_ref[...] = mm(rows, cross_ref[...], ((1,), (0,)))


def in_vmem(kernel, out_shape, flops, *operands):
    outs = len(out_shape)
    return pl.pallas_call(
        kernel,
        out_shape=out_shape,
        in_specs=[pl.BlockSpec(memory_space=pltpu.VMEM)] * len(operands),
        out_specs=(pl.BlockSpec(memory_space=pltpu.VMEM),) * outs,
        compiler_params=pltpu.CompilerParams(vmem_limit_bytes=24 * 1024 * 1024),
        cost_estimate=pl.CostEstimate(
            flops=flops, bytes_accessed=4 * sum(x.size for x in operands), transcendentals=0
        ),
    )(*operands)


def sum_kernel(orders, x_ref, out_ref, *scratch):
    lanes, steps = len(orders), len(orders[0])
    slots = [scratch[lane * steps : (lane + 1) * steps] for lane in range(lanes)]
    down_send, down_recv, up_send, up_recv = scratch[lanes * steps :]
    me = lax.axis_index("row")
    share = x_ref.shape[0] // lanes
    bits = [lax.rem(me // (1 << b), 2) for b in range(steps)]
    partners = [me + (1 - 2 * bits[b]) * (1 << b) for b in range(steps)]

    barrier = pltpu.get_barrier_semaphore()
    for partner in partners:
        pl.semaphore_signal(
            barrier, inc=1, device_id={"row": partner}, device_id_type=pl.DeviceIdType.MESH
        )
    pl.semaphore_wait(barrier, steps)

    def source(lane, step):
        return x_ref.at[pl.ds(lane * share, share)] if step == 0 else slots[lane][step - 1]

    def halve(lane, step):
        bit = orders[lane][step]
        size = share >> (step + 1)
        copy = pltpu.make_async_remote_copy(
            src_ref=source(lane, step).at[pl.ds((1 - bits[bit]) * size, size)],
            dst_ref=slots[lane][step],
            send_sem=down_send.at[lane, step],
            recv_sem=down_recv.at[lane, step],
            device_id={"row": partners[bit]},
            device_id_type=pl.DeviceIdType.MESH,
        )
        copy.start()
        return copy

    def offset(lane, level):
        total = lane * share
        for step in range(level):
            total = total + bits[orders[lane][step]] * (share >> (step + 1))
        return total

    def double(lane, step):
        bit = orders[lane][step]
        own = pl.ds(offset(lane, step + 1), share >> (step + 1))
        copy = pltpu.make_async_remote_copy(
            src_ref=out_ref.at[own],
            dst_ref=out_ref.at[own],
            send_sem=up_send.at[lane, step],
            recv_sem=up_recv.at[lane, step],
            device_id={"row": partners[bit]},
            device_id_type=pl.DeviceIdType.MESH,
        )
        copy.start()
        return copy

    flying = [halve(lane, 0) for lane in range(lanes)]
    for step in range(steps):
        for lane in range(lanes):
            flying[lane].wait()
            size = share >> (step + 1)
            kept = source(lane, step)[pl.ds(bits[orders[lane][step]] * size, size)]
            if step + 1 < steps:
                slots[lane][step][...] = slots[lane][step][...] + kept
                flying[lane] = halve(lane, step + 1)
            else:
                out_ref[pl.ds(offset(lane, steps), size)] = slots[lane][step][...] + kept
                flying[lane] = double(lane, steps - 1)
    for step in range(steps - 1, -1, -1):
        for lane in range(lanes):
            flying[lane].wait()
            if step > 0:
                flying[lane] = double(lane, step - 1)


def sum_tiles(tiles, devices):
    steps = devices.bit_length() - 1
    straight = list(range(steps))
    orders = (straight, straight[:1] + straight[2:] + straight[1:2])
    share = tiles.shape[0] // len(orders)
    slots = [
        pltpu.VMEM((share >> (step + 1),) + tiles.shape[1:], jnp.float32)
        for _ in orders
        for step in range(steps)
    ]
    sems = [pltpu.SemaphoreType.DMA((len(orders), steps))] * 4
    return pl.pallas_call(
        functools.partial(sum_kernel, orders),
        out_shape=jax.ShapeDtypeStruct(tiles.shape, jnp.float32),
        in_specs=[pl.BlockSpec(memory_space=pltpu.VMEM)],
        out_specs=pl.BlockSpec(memory_space=pltpu.VMEM),
        scratch_shapes=slots + sems,
        compiler_params=pltpu.CompilerParams(
            collective_id=0, has_side_effects=True, vmem_limit_bytes=24 * 1024 * 1024
        ),
        cost_estimate=pl.CostEstimate(
            flops=1 << 33, bytes_accessed=8 * tiles.size, transcendentals=0
        ),
    )(tiles)


def sum_gram(basis, inverse=None):
    devices = lax.axis_size("row")
    folded = folded_gram(basis, devices, inverse)
    return sum_tiles(folded.reshape(-1, 8, LANES), devices).reshape(folded.shape)


def per_device(matrix_a, matrix_b):
    width = matrix_a.shape[1]
    out_rows = width // lax.axis_size("row")
    start = lax.axis_index("row") * out_rows
    whole = jax.ShapeDtypeStruct((width, width), jnp.float32)
    share = jax.ShapeDtypeStruct((out_rows, width), jnp.float32)
    gram1 = sum_gram(matrix_a)
    (cross,) = in_vmem(
        cross_kernel, (whole,), 12 * matrix_a.shape[0] * width**2, matrix_a, matrix_b
    )
    gram1, cross = lax.optimization_barrier((gram1, cross))
    cross = lax.psum_scatter(cross, "row", scatter_dimension=0, tiled=True)
    upper1, inverse1 = factor_pair(gram1, width, True)
    gram2 = sum_gram(matrix_a, inverse1)
    gram2, cross = lax.optimization_barrier((gram2, cross))
    cross = lax.all_gather(cross, "row", axis=0, tiled=True)
    upper2, inverse2 = factor_pair(gram2, width, False)
    first_rows = lax.dynamic_slice_in_dim(upper1, start, out_rows, 0)
    second_rows = lax.dynamic_slice_in_dim(upper2, start, out_rows, 0)
    inverse_rows = lax.dynamic_slice_in_dim(inverse2, start, out_rows, 0)
    factor_rows, projection = in_vmem(
        tail_kernel,
        (share, share),
        36 * out_rows * width**2,
        second_rows,
        inverse_rows,
        upper1,
        inverse1,
        cross,
    )
    return (first_rows, factor_rows, projection)


def solution(mesh):
    placed = P(("groups", "row"), None)
    return jax.shard_map(
        per_device,
        mesh=mesh,
        in_specs=(placed, placed),
        out_specs=(placed, placed, placed),
        check_vma=False,
    )
```
